512 devices in a mesh: row: 32 (over z, core), col: 8 (over x_hi, y), dp: 2 (over x_lo).
Axes of the slice: x: 4 (x_hi: 2, x_lo: 2; x = x_hi * 2 + x_lo), y: 4, z: 16, core: 2. Of those that a mesh axis runs over, the one named last changes fastest.
Arguments:
- activations: bfloat16 [2, 1024, 25600], P('dp', 'col', 'row'), may hold values from -12 to 12
- out_grads: bfloat16 [2, 1024, 5120], P('dp', 'row', 'col'), may hold values from -12 to 12
- weight: bfloat16 [25600, 5120], P('row', 'col'), may hold values from -0.078125 to 0.078125
Outputs:
- input_grads: bfloat16 [2, 1024, 25600], P('dp', 'col', 'row')
- example_norms: float32 [2], P('dp')
- weight_grad: float32 [25600, 5120], P('row', 'col')
The draws below stay inside these ranges and needn't reach their ends.
All inputs are finite; a program needn't handle non-finite values.
Results may differ from the reference program's by a relative error of at most 0.001.
Values may be sent and summed in bfloat16 or wider, within the bound.
No kernel may reach another device: no remote copies, remote signals or barrier semaphores. Data moves between devices by JAX's collectives and lax.ppermute only.
A program may use at most 64 MiB of HBM per device.

```python
import math
import jax
import jax.numpy as jnp

FF = 25600
D = 5120
TOK = 1024
EXAMPLES = 2


def example_loudness(key, share):
    key = jax.random.fold_in(key, 5)
    flip = jax.random.randint(key, (), 0, 2)
    index = jnp.arange(EXAMPLES, dtype=jnp.int32)
    quiet = 0.3 / math.sqrt(1.0 + TOK * share * share * share * share)
    return jnp.where((index + flip) % 2 == 0, 3.0, quiet).astype(jnp.float32)


def scaled_field(key, width, spread, token_unit, token_power, loud, share):
    keys = jax.random.split(key, 4)
    shape = (EXAMPLES, TOK, width)
    normal_part = jax.random.normal(keys[0], shape, jnp.float32)
    noise = normal_part
    common_dir = jax.random.normal(keys[3], (EXAMPLES, 1, width), jnp.float32)
    base = share * common_dir + math.sqrt(1.0 - share * share) * noise
    token_scale = jnp.exp(spread * token_unit)
    token_norm = ((math.exp(token_power * spread) - 1.0) / (token_power * spread)) ** (1.0 / token_power)
    col_scale = jnp.exp(spread * jax.random.uniform(keys[2], (EXAMPLES, 1, width), jnp.float32))
    col_norm = math.sqrt((math.exp(2.0 * spread) - 1.0) / (2.0 * spread))
    value = base * token_scale * col_scale * jnp.sqrt(loud)[:, None, None] / (token_norm * col_norm)
    return jnp.clip(value, -12.0, 12.0)


def draw_activations(key, part):
    loud = example_loudness(key, 0.5)
    inner = jax.random.fold_in(key, 11)
    own = jax.random.uniform(jax.random.fold_in(inner, 3), (EXAMPLES, TOK, 1), jnp.float32)
    value = scaled_field(inner, FF, math.log(10.0), own, 2.0, loud, 0.5)
    return value.astype(jnp.bfloat16)


def draw_out_grads(key, part):
    loud = example_loudness(key, 0.5)
    inner = jax.random.fold_in(key, 23)
    own = jax.random.uniform(jax.random.fold_in(inner, 3), (EXAMPLES, TOK, 1), jnp.float32)
    value = scaled_field(inner, D, math.log(10.0), own, 2.0, loud, 0.5)
    return value.astype(jnp.bfloat16)


def shard_levels(rng, shape, cuts, low, largest):
    loudness, own = 1.0, jax.random.fold_in(rng, 6)
    for axis_at, shards_of in cuts:
        heights = jnp.exp(jax.random.uniform(jax.random.fold_in(own, axis_at), (shards_of,), jnp.float32, low / len(cuts), largest / len(cuts)))
        loudness = loudness * jnp.repeat(heights, shape[axis_at] // shards_of).reshape([-1 if axis == axis_at else 1 for axis in range(len(shape))])
    return loudness


def scatter_about(rng, shape, scale, reach, cuts=(), kind=jnp.bfloat16):
    values = scale * jax.random.normal(rng, shape, jnp.float32)
    if cuts:
        values = values * shard_levels(rng, shape, cuts, -0.22, 0.18)
    return jnp.clip(values, -reach, reach).astype(kind)


def setup_inputs(seed: int = 0) -> dict:
    key_list = jax.random.split(jax.random.key(seed), 4)
    return {
        "activations": draw_activations(jax.random.fold_in(key_list[3], 71), 0),
        "out_grads": draw_out_grads(jax.random.fold_in(key_list[3], 71), 0),
        "weight": scatter_about(key_list[2], (FF, D), D ** -0.5, 0.078125, ((0, 32), (1, 8))),
    }


def reference(activations, out_grads, weight):
    bound = math.sqrt(TOK * FF * D)
    input_list = []
    norm_list = []
    total = jnp.zeros((FF, D), jnp.float32)
    for example in range(EXAMPLES):
        hidden = activations[example]
        grads = out_grads[example]
        dh = jnp.dot(grads, weight.T, preferred_element_type=jnp.float32).astype(jnp.bfloat16)
        input_list.append(dh)
        act_gram = jnp.dot(hidden, hidden.T, preferred_element_type=jnp.float32)
        grad_gram = jnp.dot(grads, grads.T, preferred_element_type=jnp.float32)
        squared = jnp.sum(act_gram * grad_gram)
        norm_value = jnp.sqrt(squared)
        norm_list.append(norm_value)
        factor = 1.0 / jnp.maximum(1.0, norm_value / bound)
        grad_block = jnp.dot(hidden.T, grads, preferred_element_type=jnp.float32)
        total = total + factor * grad_block
    return (jnp.stack(input_list), jnp.stack(norm_list).astype(jnp.float32), total)
```

```python
import math

import jax
import jax.numpy as jnp
from jax import lax
from jax.experimental import pallas as pl
from jax.experimental.pallas import tpu as pltpu
from jax.sharding import Mesh
from jax.sharding import PartitionSpec as P

FF = 25600
D = 5120
TOK = 1024

AXES = ("za", "zb", "core", "xh", "y", "xl")
SIZES = (4, 4, 2, 2, 4, 2)
F_LOC = 800
D_LOC = 640
BF16 = jnp.bfloat16
F32 = jnp.float32
VMEM_LIMIT = 24 * 1024 * 1024


def flip(size, k):
    return [(i, i ^ k) for i in range(size)]


def dh_call(pos, mine, other, weight):
    def body(pos, mine, other, w, full, p0, p1, p2, p3):
        core, xh = pos[2], pos[3]
        for b in range(4):
            for a in range(4):
                start = ((pos[0] ^ a) * 4 + b) * 64
                here = pl.multiple_of(start + core * 32, 32)
                there = pl.multiple_of(start + (1 - core) * 32, 32)
                full[pl.ds(here, 32), :] = mine[b, a]
                full[pl.ds(there, 32), :] = other[b, a]
        weight = w[...]
        for k, out in enumerate((p0, p1, p2, p3)):
            for dx in range(2):
                start = ((xh ^ dx) * 4 + (pos[4] ^ k)) * 128
                out[dx] = lax.dot_general(
                    weight,
                    full[pl.ds(pl.multiple_of(start, 128), 128), :],
                    (((1,), (1,)), ((), ())),
                    preferred_element_type=F32,
                )

    vmem = pl.BlockSpec(memory_space=pltpu.VMEM)
    part = jax.ShapeDtypeStruct((2, F_LOC, 128), F32)
    return pl.pallas_call(
        body,
        out_shape=(jax.ShapeDtypeStruct((TOK, D_LOC), BF16),) + (part,) * 4,
        in_specs=[pl.BlockSpec(memory_space=pltpu.SMEM)] + [vmem] * 3,
        out_specs=(vmem,) * 5,
        compiler_params=pltpu.CompilerParams(vmem_limit_bytes=VMEM_LIMIT),
        cost_estimate=pl.CostEstimate(
            flops=2 * TOK * F_LOC * D_LOC, bytes_accessed=6_000_000, transcendentals=0
        ),
        name="input_grad_partials",
    )(pos, mine, other, weight)


def wg_call(hidden, full):
    def body(hidden, full, out, square):
        lhs = jnp.concatenate([hidden[j] for j in range(8)], axis=1)
        acc = jnp.dot(lhs, full[...], preferred_element_type=F32)
        out[...] = acc
        square[...] = jnp.full((8, 128), jnp.sum(acc * acc), F32)

    vmem = pl.BlockSpec(memory_space=pltpu.VMEM)
    return pl.pallas_call(
        body,
        out_shape=(
            jax.ShapeDtypeStruct((F_LOC, D_LOC), F32),
            jax.ShapeDtypeStruct((8, 128), F32),
        ),
        in_specs=[vmem] * 2,
        out_specs=(vmem,) * 2,
        compiler_params=pltpu.CompilerParams(vmem_limit_bytes=VMEM_LIMIT),
        cost_estimate=pl.CostEstimate(
            flops=2 * TOK * F_LOC * D_LOC, bytes_accessed=5_000_000, transcendentals=0
        ),
        name="weight_grad_block",
    )(hidden, full)


def local(activations, out_grads, weight):
    pos = jnp.stack([lax.axis_index(a) for a in AXES]).astype(jnp.int32)
    xl = pos[5]

    hidden = activations[0].T
    hidden_full = lax.all_to_all(
        jnp.broadcast_to(hidden[None], (8, F_LOC, 128)), ("xh", "y"), 0, 0
    )

    grads = out_grads[0]
    far = [lax.ppermute(grads, "za", flip(4, k)) for k in (1, 2, 3)]
    mine = lax.all_gather(jnp.stack([grads, *far]), "zb")
    other = lax.ppermute(mine, "core", flip(2, 1))

    full, p0, *parts = dh_call(pos, mine, other, weight)
    got = [lax.ppermute(p, "y", flip(4, k)) for k, p in zip((1, 2, 3), parts)]
    block, square = wg_call(hidden_full, full)
    peer = lax.ppermute(block, "xl", flip(2, 1))

    squared = jnp.where(jnp.arange(2) == xl, square[0, 0], 0.0)
    spread = jnp.broadcast_to(squared, (128, 2))
    squared = jnp.sum(lax.all_to_all(spread, ("za", "zb", "core", "y"), 0, 0), axis=0)
    squared, got = lax.optimization_barrier((squared, got))
    half = p0 + got[0] + got[1] + got[2]
    away = lax.ppermute(half[1], "xh", flip(2, 1))
    squared, half = lax.optimization_barrier((squared, half))
    squared = lax.psum(squared, ("xh", "xl"))
    norms = jnp.sqrt(squared)
    bound = math.sqrt(TOK * FF * D)
    factor = 1.0 / jnp.maximum(1.0, norms / bound)
    weight_grad = factor[xl] * block + factor[1 - xl] * peer

    input_grads = (half[0] + away).astype(BF16).T[None]
    return (input_grads, jnp.reshape(norms[xl], (1,)), weight_grad)


def solution(mesh):
    fine = Mesh(mesh.devices.reshape(SIZES), AXES)
    row, col = ("za", "zb", "core"), ("xh", "y")
    return jax.shard_map(
        local,
        mesh=fine,
        in_specs=(P("xl", col, row), P("xl", row, col), P(row, col)),
        out_specs=(P("xl", col, row), P("xl"), P(row, col)),
        check_vma=False,
    )
```

```python
import math

import jax
import jax.numpy as jnp
from jax import lax
from jax.experimental import pallas as pl
from jax.experimental.pallas import tpu as pltpu
from jax.sharding import Mesh
from jax.sharding import PartitionSpec as P

FF = 25600
D = 5120
TOK = 1024

AXES = ("za", "zb", "core", "xh", "y", "xl")
SIZES = (4, 4, 2, 2, 4, 2)
F_LOC = 800
D_LOC = 640
BF16 = jnp.bfloat16
F32 = jnp.float32
VMEM_LIMIT = 20 * 1024 * 1024

VMEM = pl.BlockSpec(memory_space=pltpu.VMEM)
SMEM = pl.BlockSpec(memory_space=pltpu.SMEM)
HBM = pl.BlockSpec(memory_space=pltpu.HBM)
PARAMS = pltpu.CompilerParams(vmem_limit_bytes=VMEM_LIMIT)


def flip(size, k):
    return [(i, i ^ k) for i in range(size)]


def fetch(pairs, sems):
    copies = [
        pltpu.make_async_copy(src, dst, sems.at[i]) for i, (src, dst) in enumerate(pairs)
    ]
    for copy in copies:
        copy.start()
    return copies


def block_grad(pos, hidden, mine, other):
    def body(pos, hidden, mine, other, out, square, full):
        xl, core = pos[5], pos[2]
        for b in range(4):
            for a in range(4):
                start = (a * 4 + b) * 64
                here, there = mine[b, a], other[b, a]
                full[start : start + 32, :] = jnp.where(core == 0, here, there)
                full[start + 32 : start + 64, :] = jnp.where(core == 0, there, here)
        lhs = jnp.concatenate([hidden[j] for j in range(8)], axis=1)
        acc = jnp.dot(lhs, full[...], preferred_element_type=F32)
        out[...] = acc
        total = jnp.sum(acc * acc)
        square[0] = jnp.where(xl == 0, total, 0.0)
        square[1] = jnp.where(xl == 1, total, 0.0)

    return pl.pallas_call(
        body,
        out_shape=(
            jax.ShapeDtypeStruct((F_LOC, D_LOC), F32),
            jax.ShapeDtypeStruct((2,), F32),
        ),
        in_specs=[SMEM, VMEM, VMEM, VMEM],
        out_specs=(VMEM, SMEM),
        scratch_shapes=[pltpu.VMEM((TOK, D_LOC), BF16)],
        compiler_params=PARAMS,
        cost_estimate=pl.CostEstimate(
            flops=2 * TOK * F_LOC * D_LOC, bytes_accessed=5_000_000, transcendentals=0
        ),
        name="own_weight_grad",
    )(pos, hidden, mine, other)


def input_parts(pos, mine, other, far, far_other, weight, far_weight):
    def body(pos, mine, other, far, far_other, w, far_w, p0, p1, p2, p3, near_t, far_t):
        core, xh, y = pos[2], pos[3], pos[4]
        for block in range(4):
            for i in range(2):
                zb, za = 2 * (block % 2) + i, block // 2
                start = (block ^ y) * 128 + i * 64
                here = pl.multiple_of(start + core * 32, 32)
                there = pl.multiple_of(start + (1 - core) * 32, 32)
                near_t[pl.ds(here, 32), :] = mine[zb, 2 * xh + za]
                near_t[pl.ds(there, 32), :] = other[zb, 2 * xh + za]
                far_t[pl.ds(here, 32), :] = far[zb, za]
                far_t[pl.ds(there, 32), :] = far_other[zb, za]
        dims = (((1,), (1,)), ((), ()))
        acc = lax.dot_general(w[...], near_t[...], dims, preferred_element_type=F32)
        acc += lax.dot_general(far_w[...], far_t[...], dims, preferred_element_type=F32)
        for k, out in enumerate((p0, p1, p2, p3)):
            out[...] = acc[:, k * 128 : (k + 1) * 128]

    part = jax.ShapeDtypeStruct((F_LOC, 128), F32)
    return pl.pallas_call(
        body,
        out_shape=(part,) * 4,
        in_specs=[SMEM] + [VMEM] * 6,
        out_specs=(VMEM,) * 4,
        scratch_shapes=[
            pltpu.VMEM((512, D_LOC), BF16),
            pltpu.VMEM((512, D_LOC), BF16),
        ],
        compiler_params=PARAMS,
        cost_estimate=pl.CostEstimate(
            flops=2 * TOK * F_LOC * D_LOC, bytes_accessed=6_000_000, transcendentals=0
        ),
        name="input_grad_partials",
    )(pos, mine, other, far, far_other, weight, far_weight)


CHUNKS = 5
ROWS = F_LOC // CHUNKS


def combine(pos, squared, block, peer):
    bound = math.sqrt(TOK * FF * D)

    def body(pos, squared, block, peer, out, b_buf, p_buf, o_buf, sems, out_sems):
        parts = [pl.ds(i * ROWS, ROWS) for i in range(CHUNKS)]
        copies = fetch(
            [(src.at[p], buf.at[p]) for p in parts for src, buf in ((block, b_buf), (peer, p_buf))],
            sems,
        )
        xl = pos[5]
        values = [jnp.full((1, D_LOC), squared[i], F32) for i in range(2)]
        factors = [1.0 / jnp.maximum(1.0, jnp.sqrt(v) / bound) for v in values]
        own = jnp.where(xl == 0, factors[0], factors[1])
        next_ = jnp.where(xl == 0, factors[1], factors[0])
        stores = []
        for i, p in enumerate(parts):
            copies[2 * i].wait()
            copies[2 * i + 1].wait()
            o_buf[p] = own * b_buf[p] + next_ * p_buf[p]
            store = pltpu.make_async_copy(o_buf.at[p], out.at[p], out_sems.at[i])
            store.start()
            stores.append(store)
        for store in stores:
            store.wait()

    buf = pltpu.VMEM((F_LOC, D_LOC), F32)
    return pl.pallas_call(
        body,
        out_shape=jax.ShapeDtypeStruct((F_LOC, D_LOC), F32),
        in_specs=[SMEM, SMEM, HBM, HBM],
        out_specs=HBM,
        scratch_shapes=[
            buf,
            buf,
            buf,
            pltpu.SemaphoreType.DMA((2 * CHUNKS,)),
            pltpu.SemaphoreType.DMA((CHUNKS,)),
        ],
        compiler_params=PARAMS,
        cost_estimate=pl.CostEstimate(
            flops=3 * F_LOC * D_LOC, bytes_accessed=6_000_000, transcendentals=0
        ),
        name="combine",
    )(pos, squared, block, peer)


def local(activations, out_grads, weight):
    pos = jnp.stack([lax.axis_index(a) for a in AXES]).astype(jnp.int32)
    xh, xl = pos[3], pos[5]

    hidden = lax.all_to_all(
        jnp.broadcast_to(activations[0].T[None], (8, F_LOC, 128)), ("xh", "y"), 0, 0
    )
    far_weight = lax.ppermute(weight, ("xh", "xl"), [(i, 3 - i) for i in range(4)])

    mine = lax.all_gather(lax.all_gather(out_grads[0], "za"), "zb")
    other = lax.ppermute(mine, "core", flip(2, 1))
    away = lax.dynamic_slice_in_dim(mine, 2 * (1 - xh), 2, axis=1)
    far = lax.ppermute(away, "xh", flip(2, 1))

    other, far_weight = lax.optimization_barrier((other, far_weight))
    block, squared = block_grad(pos, hidden, mine, other)
    squared = lax.psum(squared, ("xh", "xl"))
    far, squared, block = lax.optimization_barrier((far, squared, block))
    next_block = lax.ppermute(block, "xl", flip(2, 1))
    far_other = lax.ppermute(far, "core", flip(2, 1))
    p0, *parts = input_parts(pos, mine, other, far, far_other, weight, far_weight)
    squared, p0 = lax.optimization_barrier((squared, p0))
    got = [lax.ppermute(p, "y", flip(4, k)) for k, p in zip((1, 2, 3), parts)]
    input_grads = (p0 + got[0] + got[1] + got[2]).astype(BF16).T[None]

    spread = jnp.broadcast_to(squared, (128, 2))
    squared = jnp.sum(lax.all_to_all(spread, ("za", "zb", "core", "y"), 0, 0), axis=0)
    norms = jnp.sqrt(squared)
    weight_grad = combine(pos, squared, block, next_block)
    return (input_grads, jnp.reshape(norms[xl], (1,)), weight_grad)


def solution(mesh):
    fine = Mesh(mesh.devices.reshape(SIZES), AXES)
    row, col = ("za", "zb", "core"), ("xh", "y")
    return jax.shard_map(
        local,
        mesh=fine,
        in_specs=(P("xl", col, row), P("xl", row, col), P(row, col)),
        out_specs=(P("xl", col, row), P("xl"), P(row, col)),
        check_vma=False,
    )
```

```python
import math

import jax
import jax.numpy as jnp
from jax import lax
from jax.experimental import pallas as pl
from jax.experimental.pallas import tpu as pltpu
from jax.sharding import Mesh
from jax.sharding import PartitionSpec as P

FF = 25600
D = 5120
TOK = 1024

AXES = ("za", "zb", "core", "xh", "y", "xl")
SIZES = (4, 4, 2, 2, 4, 2)
F_LOC = 800
D_LOC = 640
BF16 = jnp.bfloat16
F32 = jnp.float32
VMEM_LIMIT = 20 * 1024 * 1024

VMEM = pl.BlockSpec(memory_space=pltpu.VMEM)
SMEM = pl.BlockSpec(memory_space=pltpu.SMEM)
HBM = pl.BlockSpec(memory_space=pltpu.HBM)
PARAMS = pltpu.CompilerParams(vmem_limit_bytes=VMEM_LIMIT)


def flip(size, k):
    return [(i, i ^ k) for i in range(size)]


def fetch(pairs, sems):
    copies = [
        pltpu.make_async_copy(src, dst, sems.at[i]) for i, (src, dst) in enumerate(pairs)
    ]
    for copy in copies:
        copy.start()
    return copies


def block_grad(pos, hidden, mine, other):
    def body(pos, hidden, mine, other, out, square, full):
        xl, core = pos[5], pos[2]
        for b in range(4):
            for a in range(4):
                start = (a * 4 + b) * 64
                here, there = mine[b, a], other[b, a]
                full[start : start + 32, :] = jnp.where(core == 0, here, there)
                full[start + 32 : start + 64, :] = jnp.where(core == 0, there, here)
        lhs = jnp.concatenate([hidden[j] for j in range(8)], axis=1)
        acc = jnp.dot(lhs, full[...], preferred_element_type=F32)
        out[...] = acc
        total = jnp.sum(acc * acc)
        square[0] = jnp.where(xl == 0, total, 0.0)
        square[1] = jnp.where(xl == 1, total, 0.0)

    return pl.pallas_call(
        body,
        out_shape=(
            jax.ShapeDtypeStruct((F_LOC, D_LOC), F32),
            jax.ShapeDtypeStruct((2,), F32),
        ),
        in_specs=[SMEM, VMEM, VMEM, VMEM],
        out_specs=(VMEM, SMEM),
        scratch_shapes=[pltpu.VMEM((TOK, D_LOC), BF16)],
        compiler_params=PARAMS,
        cost_estimate=pl.CostEstimate(
            flops=2 * TOK * F_LOC * D_LOC, bytes_accessed=5_000_000, transcendentals=0
        ),
        name="own_weight_grad",
    )(pos, hidden, mine, other)


def input_parts(pos, mine, other, far, far_other, weight, far_weight):
    def body(pos, mine, other, far, far_other, w, far_w, p0, p1, p2, p3, near_t, far_t):
        core, xh, y = pos[2], pos[3], pos[4]
        for block in range(4):
            for i in range(2):
                zb, za = 2 * (block % 2) + i, block // 2
                start = (block ^ y) * 128 + i * 64
                here = pl.multiple_of(start + core * 32, 32)
                there = pl.multiple_of(start + (1 - core) * 32, 32)
                near_t[pl.ds(here, 32), :] = mine[zb, 2 * xh + za]
                near_t[pl.ds(there, 32), :] = other[zb, 2 * xh + za]
                far_t[pl.ds(here, 32), :] = far[zb, za]
                far_t[pl.ds(there, 32), :] = far_other[zb, za]
        dims = (((1,), (1,)), ((), ()))
        acc = lax.dot_general(w[...], near_t[...], dims, preferred_element_type=F32)
        acc += lax.dot_general(far_w[...], far_t[...], dims, preferred_element_type=F32)
        for k, out in enumerate((p0, p1, p2, p3)):
            out[...] = acc[:, k * 128 : (k + 1) * 128]

    part = jax.ShapeDtypeStruct((F_LOC, 128), F32)
    return pl.pallas_call(
        body,
        out_shape=(part,) * 4,
        in_specs=[SMEM] + [VMEM] * 6,
        out_specs=(VMEM,) * 4,
        scratch_shapes=[
            pltpu.VMEM((512, D_LOC), BF16),
            pltpu.VMEM((512, D_LOC), BF16),
        ],
        compiler_params=PARAMS,
        cost_estimate=pl.CostEstimate(
            flops=2 * TOK * F_LOC * D_LOC, bytes_accessed=6_000_000, transcendentals=0
        ),
        name="input_grad_partials",
    )(pos, mine, other, far, far_other, weight, far_weight)


CHUNKS = 5
ROWS = F_LOC // CHUNKS


def combine(pos, squared, block, peer, parts):
    bound = math.sqrt(TOK * FF * D)

    def body(
        pos, squared, block, peer, q0, q1, q2, q3, out, tokens, norm,
        b_buf, p_buf, o_buf, q_buf, sems, out_sems,
    ):
        rows = [pl.ds(i * ROWS, ROWS) for i in range(CHUNKS)]
        pairs = [(q, q_buf.at[i]) for i, q in enumerate((q0, q1, q2, q3))]
        for r in rows:
            pairs += [(block.at[r], b_buf.at[r]), (peer.at[r], p_buf.at[r])]
        copies = fetch(pairs, sems)
        xl = pos[5]
        norms = [jnp.sqrt(jnp.full((8, D_LOC), squared[i], F32)) for i in range(2)]
        factors = [(1.0 / jnp.maximum(1.0, v / bound))[:1] for v in norms]
        own = jnp.where(xl == 0, factors[0], factors[1])
        next_ = jnp.where(xl == 0, factors[1], factors[0])
        norm[0] = jnp.max(jnp.where(xl == 0, norms[0], norms[1]))
        for copy in copies[:4]:
            copy.wait()
        tokens[...] = (q_buf[0] + q_buf[1] + q_buf[2] + q_buf[3]).astype(BF16)
        stores = []
        for i, r in enumerate(rows):
            copies[4 + 2 * i].wait()
            copies[5 + 2 * i].wait()
            o_buf[r] = own * b_buf[r] + next_ * p_buf[r]
            store = pltpu.make_async_copy(o_buf.at[r], out.at[r], out_sems.at[i])
            store.start()
            stores.append(store)
        for store in stores:
            store.wait()

    buf = pltpu.VMEM((F_LOC, D_LOC), F32)
    return pl.pallas_call(
        body,
        out_shape=(
            jax.ShapeDtypeStruct((F_LOC, D_LOC), F32),
            jax.ShapeDtypeStruct((F_LOC, 128), BF16),
            jax.ShapeDtypeStruct((1,), F32),
        ),
        in_specs=[SMEM, SMEM] + [HBM] * 6,
        out_specs=(HBM, VMEM, SMEM),
        scratch_shapes=[
            buf,
            buf,
            buf,
            pltpu.VMEM((4, F_LOC, 128), F32),
            pltpu.SemaphoreType.DMA((4 + 2 * CHUNKS,)),
            pltpu.SemaphoreType.DMA((CHUNKS,)),
        ],
        compiler_params=PARAMS,
        cost_estimate=pl.CostEstimate(
            flops=3 * F_LOC * D_LOC, bytes_accessed=8_000_000, transcendentals=0
        ),
        name="combine",
    )(pos, squared, block, peer, *parts)


def local(activations, out_grads, weight):
    pos = jnp.stack([lax.axis_index(a) for a in AXES]).astype(jnp.int32)
    xh = pos[3]

    hidden = lax.all_to_all(
        jnp.broadcast_to(activations[0].T[None], (8, F_LOC, 128)), ("xh", "y"), 0, 0
    )
    far_weight = lax.ppermute(weight, ("xh", "xl"), [(i, 3 - i) for i in range(4)])

    mine = lax.all_gather(lax.all_gather(out_grads[0], "za"), "zb")
    other = lax.ppermute(mine, "core", flip(2, 1))
    away = lax.dynamic_slice_in_dim(mine, 2 * (1 - xh), 2, axis=1)
    far = lax.ppermute(away, "xh", flip(2, 1))

    other, far_weight = lax.optimization_barrier((other, far_weight))
    block, squared = block_grad(pos, hidden, mine, other)
    squared = lax.psum(squared, ("xh", "xl"))
    far, squared, block = lax.optimization_barrier((far, squared, block))
    next_block = lax.ppermute(block, "xl", flip(2, 1))
    far_other = lax.ppermute(far, "core", flip(2, 1))
    p0, *parts = input_parts(pos, mine, other, far, far_other, weight, far_weight)
    squared, p0 = lax.optimization_barrier((squared, p0))
    got = [lax.ppermute(p, "y", flip(4, k)) for k, p in zip((1, 2, 3), parts)]

    spread = jnp.broadcast_to(squared, (128, 2))
    squared = jnp.sum(lax.all_to_all(spread, ("za", "zb", "core", "y"), 0, 0), axis=0)
    weight_grad, tokens, norm = combine(pos, squared, block, next_block, (p0, *got))
    return (tokens.T[None], norm, weight_grad)


def solution(mesh):
    fine = Mesh(mesh.devices.reshape(SIZES), AXES)
    row, col = ("za", "zb", "core"), ("xh", "y")
    return jax.shard_map(
        local,
        mesh=fine,
        in_specs=(P("xl", col, row), P("xl", row, col), P(row, col)),
        out_specs=(P("xl", col, row), P("xl"), P(row, col)),
        check_vma=False,
    )
```

```python
import math

import jax
import jax.numpy as jnp
from jax import lax
from jax.experimental import pallas as pl
from jax.experimental.pallas import tpu as pltpu
from jax.sharding import Mesh
from jax.sharding import PartitionSpec as P

FF = 25600
D = 5120
TOK = 1024

AXES = ("za", "zb", "core", "xh", "y", "xl")
SIZES = (4, 4, 2, 2, 4, 2)
F_LOC = 800
D_LOC = 640
BF16 = jnp.bfloat16
F32 = jnp.float32
VMEM_LIMIT = 20 * 1024 * 1024

VMEM = pl.BlockSpec(memory_space=pltpu.VMEM)
SMEM = pl.BlockSpec(memory_space=pltpu.SMEM)
HBM = pl.BlockSpec(memory_space=pltpu.HBM)
PARAMS = pltpu.CompilerParams(vmem_limit_bytes=VMEM_LIMIT)


def flip(size, k):
    return [(i, i ^ k) for i in range(size)]


def fetch(pairs, sems):
    copies = [
        pltpu.make_async_copy(src, dst, sems.at[i]) for i, (src, dst) in enumerate(pairs)
    ]
    for copy in copies:
        copy.start()
    return copies


def block_grad(pos, hidden, mine, other):
    def body(pos, hidden, mine, other, out, square, full):
        xl, core = pos[5], pos[2]
        for b in range(4):
            for a in range(4):
                start = (a * 4 + b) * 64
                here, there = mine[b, a], other[b, a]
                full[start : start + 32, :] = jnp.where(core == 0, here, there)
                full[start + 32 : start + 64, :] = jnp.where(core == 0, there, here)
        lhs = jnp.concatenate([hidden[j] for j in range(8)], axis=1)
        acc = jnp.dot(lhs, full[...], preferred_element_type=F32)
        out[...] = acc
        total = jnp.sum(acc * acc)
        square[0] = jnp.where(xl == 0, total, 0.0)
        square[1] = jnp.where(xl == 1, total, 0.0)

    return pl.pallas_call(
        body,
        out_shape=(
            jax.ShapeDtypeStruct((F_LOC, D_LOC), F32),
            jax.ShapeDtypeStruct((2,), F32),
        ),
        in_specs=[SMEM, VMEM, VMEM, VMEM],
        out_specs=(VMEM, SMEM),
        scratch_shapes=[pltpu.VMEM((TOK, D_LOC), BF16)],
        compiler_params=PARAMS,
        cost_estimate=pl.CostEstimate(
            flops=2 * TOK * F_LOC * D_LOC, bytes_accessed=5_000_000, transcendentals=0
        ),
        name="own_weight_grad",
    )(pos, hidden, mine, other)


def input_parts(pos, mine, other, far, far_other, weight, far_weight):
    def body(pos, mine, other, far, far_other, w, far_w, p0, p1, p2, p3, near_t, far_t):
        core, xh, y = pos[2], pos[3], pos[4]
        for block in range(4):
            for i in range(2):
                zb, za = 2 * (block % 2) + i, block // 2
                start = (block ^ y) * 128 + i * 64
                here = pl.multiple_of(start + core * 32, 32)
                there = pl.multiple_of(start + (1 - core) * 32, 32)
                near_t[pl.ds(here, 32), :] = mine[zb, 2 * xh + za]
                near_t[pl.ds(there, 32), :] = other[zb, 2 * xh + za]
                far_t[pl.ds(here, 32), :] = far[zb, za]
                far_t[pl.ds(there, 32), :] = far_other[zb, za]
        dims = (((1,), (1,)), ((), ()))
        acc = lax.dot_general(w[...], near_t[...], dims, preferred_element_type=F32)
        acc += lax.dot_general(far_w[...], far_t[...], dims, preferred_element_type=F32)
        for k, out in enumerate((p0, p1, p2, p3)):
            out[...] = acc[:, k * 128 : (k + 1) * 128]

    part = jax.ShapeDtypeStruct((F_LOC, 128), F32)
    return pl.pallas_call(
        body,
        out_shape=(part,) * 4,
        in_specs=[SMEM] + [VMEM] * 6,
        out_specs=(VMEM,) * 4,
        scratch_shapes=[
            pltpu.VMEM((512, D_LOC), BF16),
            pltpu.VMEM((512, D_LOC), BF16),
        ],
        compiler_params=PARAMS,
        cost_estimate=pl.CostEstimate(
            flops=2 * TOK * F_LOC * D_LOC, bytes_accessed=6_000_000, transcendentals=0
        ),
        name="input_grad_partials",
    )(pos, mine, other, far, far_other, weight, far_weight)


CHUNKS = 10
ROWS = F_LOC // CHUNKS


def combine(pos, squared, block, peer, parts):
    bound = math.sqrt(TOK * FF * D)

    def body(
        pos, squared, block, peer, q0, q1, q2, q3, out, tokens, norm,
        b_buf, p_buf, o_buf, q_buf, sems, out_sems,
    ):
        rows = [pl.ds(i * ROWS, ROWS) for i in range(CHUNKS)]
        pairs = []
        for r in rows:
            pairs += [(block.at[r], b_buf.at[r]), (peer.at[r], p_buf.at[r])]
        pairs += [(q, q_buf.at[i]) for i, q in enumerate((q0, q1, q2, q3))]
        copies = fetch(pairs, sems)
        xl = pos[5]
        norms = [jnp.sqrt(jnp.full((8, D_LOC), squared[i], F32)) for i in range(2)]
        factors = [(1.0 / jnp.maximum(1.0, v / bound))[:1] for v in norms]
        own = jnp.where(xl == 0, factors[0], factors[1])
        next_ = jnp.where(xl == 0, factors[1], factors[0])
        norm[0] = jnp.max(jnp.where(xl == 0, norms[0], norms[1]))
        stores = []
        for i, r in enumerate(rows):
            copies[2 * i].wait()
            copies[2 * i + 1].wait()
            o_buf[r] = own * b_buf[r] + next_ * p_buf[r]
            store = pltpu.make_async_copy(o_buf.at[r], out.at[r], out_sems.at[i])
            store.start()
            stores.append(store)
        for copy in copies[2 * CHUNKS :]:
            copy.wait()
        tokens[...] = (q_buf[0] + q_buf[1] + q_buf[2] + q_buf[3]).astype(BF16)
        for store in stores:
            store.wait()

    buf = pltpu.VMEM((F_LOC, D_LOC), F32)
    return pl.pallas_call(
        body,
        out_shape=(
            jax.ShapeDtypeStruct((F_LOC, D_LOC), F32),
            jax.ShapeDtypeStruct((F_LOC, 128), BF16),
            jax.ShapeDtypeStruct((1,), F32),
        ),
        in_specs=[SMEM, SMEM] + [HBM] * 6,
        out_specs=(HBM, VMEM, SMEM),
        scratch_shapes=[
            buf,
            buf,
            buf,
            pltpu.VMEM((4, F_LOC, 128), F32),
            pltpu.SemaphoreType.DMA((4 + 2 * CHUNKS,)),
            pltpu.SemaphoreType.DMA((CHUNKS,)),
        ],
        compiler_params=PARAMS,
        cost_estimate=pl.CostEstimate(
            flops=3 * F_LOC * D_LOC, bytes_accessed=8_000_000, transcendentals=0
        ),
        name="combine",
    )(pos, squared, block, peer, *parts)


def local(activations, out_grads, weight):
    pos = jnp.stack([lax.axis_index(a) for a in AXES]).astype(jnp.int32)
    xh = pos[3]

    hidden = lax.all_to_all(
        jnp.broadcast_to(activations[0].T[None], (8, F_LOC, 128)), ("xh", "y"), 0, 0
    )
    far_weight = lax.ppermute(weight, ("xh", "xl"), [(i, 3 - i) for i in range(4)])

    mine = lax.all_gather(lax.all_gather(out_grads[0], "za"), "zb")
    other = lax.ppermute(mine, "core", flip(2, 1))
    away = lax.dynamic_slice_in_dim(mine, 2 * (1 - xh), 2, axis=1)
    far = lax.ppermute(away, "xh", flip(2, 1))

    other, far_weight = lax.optimization_barrier((other, far_weight))
    block, squared = block_grad(pos, hidden, mine, other)
    squared = lax.psum(squared, ("xh", "xl"))
    far, squared, block = lax.optimization_barrier((far, squared, block))
    next_block = lax.ppermute(block, "xl", flip(2, 1))
    far_other = lax.ppermute(far, "core", flip(2, 1))
    p0, *parts = input_parts(pos, mine, other, far, far_other, weight, far_weight)
    squared, p0 = lax.optimization_barrier((squared, p0))
    got = [lax.ppermute(p, "y", flip(4, k)) for k, p in zip((1, 2, 3), parts)]

    spread = jnp.broadcast_to(squared, (128, 2))
    squared = jnp.sum(lax.all_to_all(spread, ("za", "zb", "core", "y"), 0, 0), axis=0)
    weight_grad, tokens, norm = combine(pos, squared, block, next_block, (p0, *got))
    return (tokens.T[None], norm, weight_grad)


def solution(mesh):
    fine = Mesh(mesh.devices.reshape(SIZES), AXES)
    row, col = ("za", "zb", "core"), ("xh", "y")
    return jax.shard_map(
        local,
        mesh=fine,
        in_specs=(P("xl", col, row), P("xl", row, col), P(row, col)),
        out_specs=(P("xl", col, row), P("xl"), P(row, col)),
        check_vma=False,
    )
```
